32 devices in a mesh: groups: 2 (over y), lat: 4 (over z), chan: 2 (over x), lon: 2 (over core).
Axes of the slice: x: 2, y: 2, z: 4, core: 2. Of those that a mesh axis runs over, the one named last changes fastest.
Arguments:
- activations: bfloat16 [32, 192, 512], P(('groups', 'lat'), 'lon', 'chan'), parts along dimension 0, may hold values from -6 to 6
- cotangent: bfloat16 [32, 192, 512], P(('groups', 'lat'), 'lon', 'chan'), parts along dimension 0, may hold values from -6 to 6
- w_first: bfloat16 [3, 512, 512], P(None, None, 'chan'), may hold values from -0.15625 to 0.15625
- w_second: bfloat16 [3, 512, 512], P(None, None, 'chan'), may hold values from -0.15625 to 0.15625
- offsets: int32 [16, 6], replicated, may hold values from -1 to 1, as said below
- basis: int32 [16, 6], replicated, may hold values from 0 to 2
- live: int32 [16], replicated, may hold values from 2 to 6, as said below
- taps: float32 [16, 6, 3], replicated, may hold values from -3 to 3
Outputs:
- mixed_out: bfloat16 [32, 192, 512], P(('groups', 'lat'), 'lon', 'chan'), parts along dimension 0
- grad_input: float32 [32, 192, 512], P(('groups', 'lat'), 'lon', 'chan'), parts along dimension 0
- grad_first: float32 [6, 512, 512], P('groups', None, 'chan'), parts along dimension 0
- grad_second: float32 [6, 512, 512], P('groups', None, 'chan'), parts along dimension 0
The draws below stay inside these ranges and needn't reach their ends.
There are 2 independent parts, one for each index of `groups`. The reference program is written for one: setup_inputs(seed, part) draws one part's arguments, and reference() takes and returns one part's arrays. A program takes and returns all parts, laid end to end along the dimension named above; an argument that names none is the same for every part. Nothing has to cross between parts.
Inputs may be any that keep to these rules, and one draw needn't show every extreme that they name: Row i + offsets[i, s] lies in the grid for every entry; row 8 has entries at both ends of the reach. `live`: every row i with min(i, 15 - i) < max(2, 1) uses all 6 entries; row 8 uses exactly 2.
All inputs are finite; a program needn't handle non-finite values.
Results may differ from the reference program's by a relative error of at most 0.012.
Values may be sent and summed in bfloat16 or wider, within the bound.
A program may use at most 64 MiB of HBM per device.

```python
import jax
import jax.numpy as jnp
from jax import lax

CHANNELS = 512
KB = 3
HALO = 1
SLOTS = 6
NLAT = 16
NLON = 192


def draw_offsets(key, part):
    key = jax.random.fold_in(key, 11)
    sampled = jax.random.randint(key, (NLAT, SLOTS), -HALO, HALO + 1)
    row_index = jnp.arange(NLAT)[:, None]
    column_index = jnp.arange(SLOTS)[None, :]
    middle = row_index == NLAT // 2
    sampled = jnp.where(middle & (column_index == 0), -HALO, sampled)
    sampled = jnp.where(middle & (column_index == 1), HALO, sampled)
    lower = jnp.maximum(-HALO, -row_index)
    upper = jnp.minimum(HALO, NLAT - 1 - row_index)
    return jnp.clip(sampled, lower, upper).astype(jnp.int32)


def draw_live(key, part):
    key = jax.random.fold_in(key, 13)
    sampled = jax.random.randint(key, (NLAT,), 2, SLOTS + 1)
    row_index = jnp.arange(NLAT)
    polar = jnp.minimum(row_index, NLAT - 1 - row_index) < max(NLAT // 8, 1)
    sampled = jnp.where(polar, SLOTS, sampled)
    return jnp.where(row_index == NLAT // 2, 2, sampled).astype(jnp.int32)


def touch_ends(values, rng, smallest, largest):
    longest = values.shape.index(max(values.shape))
    spots = []
    for shift in (0, 1):
        where = [jax.random.randint(jax.random.fold_in(rng, axis), (), 0, length) for axis, length in enumerate(values.shape)]
        where[longest] = (where[longest] + shift) % values.shape[longest]
        spots.append(tuple(where))
    return values.at[spots[0]].set(smallest).at[spots[1]].set(largest)


def shard_levels(stream_key, extent, pieces, least, largest):
    def one(axis_at, blocks):
        steps = jax.random.uniform(jax.random.fold_in(jax.random.fold_in(stream_key, 6), axis_at), (blocks,), jnp.float32, least / len(pieces), largest / len(pieces))
        return jnp.repeat(jnp.exp(steps), extent[axis_at] // blocks).reshape((-1,) + (1,) * (len(extent) - axis_at - 1))

    loudness = one(*pieces[0])
    for cut in pieces[1:]:
        loudness = loudness * one(*cut)
    return loudness


def gaussian(stream_key, dims, width, bound, pieces=(), dtype=jnp.bfloat16):
    drawn = width * jax.random.normal(stream_key, dims, jnp.float32)
    if pieces:
        drawn = drawn * shard_levels(stream_key, dims, pieces, -0.22, 0.18)
    return jnp.clip(drawn, -bound, bound).astype(dtype)


def setup_inputs(seed: int = 0, part: int = 0) -> dict:
    arg_keys = jax.random.split(jax.random.key(seed), 9)
    own_keys = jax.random.split(jax.random.fold_in(arg_keys[8], part), 9)
    return {
        "activations": gaussian(own_keys[0], (NLAT, NLON, CHANNELS), 1.0, 6.0, ((0, 4), (1, 2), (2, 2))),
        "cotangent": gaussian(own_keys[1], (NLAT, NLON, CHANNELS), 1.0, 6.0, ((0, 4), (1, 2), (2, 2))),
        "w_first": gaussian(arg_keys[2], (KB, CHANNELS, CHANNELS), (KB * CHANNELS) ** -0.5, 0.15625, ((2, 2),)),
        "w_second": gaussian(arg_keys[3], (KB, CHANNELS, CHANNELS), (KB * CHANNELS) ** -0.5, 0.15625, ((2, 2),)),
        "offsets": draw_offsets(jax.random.fold_in(arg_keys[8], 71), part),
        "basis": touch_ends(jax.random.randint(arg_keys[5], (NLAT, SLOTS), 0, KB), jax.random.fold_in(arg_keys[5], 1), 0, KB - 1).astype(jnp.int32),
        "live": draw_live(jax.random.fold_in(arg_keys[8], 71), part),
        "taps": gaussian(arg_keys[7], (NLAT, SLOTS, 2 * HALO + 1), 0.5, 3.0, (), jnp.float32),
    }


def coefficients(offsets, basis, live, taps):
    stencil = 2 * HALO + 1
    slot_count = offsets.shape[1]
    in_use = jnp.arange(slot_count)[None, :] < live[:, None]
    row_hit = (offsets[:, :, None] == (jnp.arange(stencil) - HALO)[None, None, :]) & in_use[:, :, None]
    kind_hit = basis[:, :, None] == jnp.arange(KB)[None, None, :]
    chosen = row_hit[:, :, :, None] & kind_hit[:, :, None, :]
    return lax.optimization_barrier(jnp.sum(jnp.where(chosen[..., None], taps[:, :, None, None, :], jnp.float32(0.0)), axis=1))

def spread(extended, coef_table):
    row_count = coef_table.shape[0]
    lon_count = extended.shape[1] - 2 * HALO
    stencil = 2 * HALO + 1
    summed = jnp.zeros((row_count, lon_count, KB, extended.shape[2]), jnp.float32)
    for shift_row in range(stencil):
        for shift_col in range(stencil):
            segment = extended[shift_row:shift_row + row_count, shift_col:shift_col + lon_count, :]
            factor = coef_table[:, shift_row, :, shift_col]
            summed = summed + factor[:, None, :, None] * segment[:, :, None, :].astype(jnp.float32)
    return summed

def spread_back(extended, coef_table):
    row_count = extended.shape[0] - 2 * HALO
    lon_count = extended.shape[1] - 2 * HALO
    stencil = 2 * HALO + 1
    summed = jnp.zeros((row_count, lon_count, extended.shape[3]), jnp.float32)
    for shift_row in range(stencil):
        for shift_col in range(stencil):
            base_row = 2 * HALO - shift_row
            base_col = 2 * HALO - shift_col
            segment = extended[base_row:base_row + row_count, base_col:base_col + lon_count]
            factor = coef_table[base_row:base_row + row_count, shift_row, :, shift_col]
            summed = summed + lax.optimization_barrier(jnp.sum(factor[:, None, :, None] * segment.astype(jnp.float32), axis=2))
    return summed

def extend(state_field):
    columns = jnp.concatenate([state_field[:, -HALO:], state_field, state_field[:, :HALO]], axis=1)
    widths = [(HALO, HALO)] + [(0, 0)] * (state_field.ndim - 1)
    return jnp.pad(columns, widths)

def reference(activations, cotangent, w_first, w_second, offsets, basis, live, taps):
    coef_table = coefficients(offsets, basis, live, taps)
    padded_table = jnp.pad(coef_table, ((HALO, HALO), (0, 0), (0, 0), (0, 0)))
    weights = (w_first, w_second)
    saved = []
    state_field = activations
    for layer_index in range(2):
        gathered = spread(extend(state_field), coef_table).astype(jnp.bfloat16)
        mixed_pre = jnp.dot(gathered.reshape(-1, KB * CHANNELS), weights[layer_index].reshape(KB * CHANNELS, CHANNELS), preferred_element_type=jnp.float32).reshape(NLAT, NLON, CHANNELS)
        saved.append((gathered, mixed_pre))
        state_field = (state_field.astype(jnp.float32) + jax.nn.gelu(mixed_pre)).astype(jnp.bfloat16)
    mixed_out = state_field
    upstream = cotangent
    grad_sums = [None, None]
    grad_input = None
    for layer_index in (1, 0):
        gathered, mixed_pre = saved[layer_index]
        gelu_grad = jax.vjp(jax.nn.gelu, mixed_pre)[1](upstream.astype(jnp.float32))[0]
        dpre = gelu_grad.astype(jnp.bfloat16)
        grad_sums[layer_index] = lax.dot_general(gathered.reshape(-1, KB * CHANNELS), dpre.reshape(-1, CHANNELS), (((0,), (0,)), ((), ())), preferred_element_type=jnp.float32).reshape(KB, CHANNELS, CHANNELS)
        dfilter = lax.dot_general(dpre.reshape(-1, CHANNELS), weights[layer_index].reshape(KB * CHANNELS, CHANNELS), (((1,), (1,)), ((), ())), preferred_element_type=jnp.float32)
        dfilter = dfilter.reshape(NLAT, NLON, KB, CHANNELS).astype(jnp.bfloat16)
        adjoint = spread_back(extend(dfilter), padded_table)
        combined = upstream.astype(jnp.float32) + adjoint
        if layer_index == 1:
            upstream = combined.astype(jnp.bfloat16)
        else:
            grad_input = combined
    return (mixed_out, grad_input, grad_sums[0], grad_sums[1])
```

```python
import functools
import math

import jax
import jax.numpy as jnp
from jax import lax
from jax.experimental import pallas as pl
from jax.experimental.pallas import tpu as pltpu
from jax.sharding import PartitionSpec as P

KB = 3
HALO = 1
EDGE = 16
MESH = pl.DeviceIdType.MESH
BF16 = jnp.bfloat16
F32 = jnp.float32
GELU_C = math.sqrt(2.0 / math.pi)
GELU_A = 0.044715


def coefficients(offsets, basis, live, taps):
    stencil = 2 * HALO + 1
    slot_count = offsets.shape[1]
    in_use = jnp.arange(slot_count)[None, :] < live[:, None]
    row_hit = (offsets[:, :, None] == (jnp.arange(stencil) - HALO)[None, None, :]) & in_use[
        :, :, None
    ]
    kind_hit = basis[:, :, None] == jnp.arange(KB)[None, None, :]
    chosen = row_hit[:, :, :, None] & kind_hit[:, :, None, :]
    return jnp.sum(
        jnp.where(chosen[..., None], taps[:, :, None, None, :], jnp.float32(0.0)), axis=1
    )


def gelu(x):
    th = jnp.tanh(GELU_C * (x + GELU_A * (x * x * x)))
    return 0.5 * x * (1.0 + th)


def gelu_slope(x):
    sq = x * x
    th = jnp.tanh(GELU_C * (x + GELU_A * (sq * x)))
    return 0.5 * (1.0 + th) + (0.5 * x) * (1.0 - th * th) * (
        GELU_C * (1.0 + (3.0 * GELU_A) * sq)
    )


def kernel(
    sizes, tab, act, cot, w1, w2, mixed, gin, g1, g2,
    ext, wb, band, v1, v2, vb, pre1, back, part, rs_out, rs_in, tot,
    s_right, r_right, s_left, r_left, ag_out, ag_in,
    x_send, x_recv, w_send, w_recv, f_send, f_recv, rs_send, rs_recv, c_send, c_recv,
    ag_send, ag_recv,
):
    nlat, nchan, nlon, chunks = sizes
    rows, cols, width = act.shape
    channels = nchan * width
    wide = cols + 2 * EDGE
    lat, chan, lon = lax.axis_index("lat"), lax.axis_index("chan"), lax.axis_index("lon")
    has_up, has_down = lat > 0, lat < nlat - 1
    mid = pl.ds(EDGE, cols)

    @pl.when(lat == 0)
    def _():
        ext[:, :, 0] = jnp.zeros(ext.shape[:2] + ext.shape[3:], BF16)

    @pl.when(lat == nlat - 1)
    def _():
        ext[:, :, rows + 1] = jnp.zeros(ext.shape[:2] + ext.shape[3:], BF16)

    barrier = pltpu.get_barrier_semaphore()

    def chan_at(step):
        return lax.rem(chan + step + nchan, nchan)

    def lon_at(step):
        return lax.rem(lon + step + nlon, nlon)

    for step in range(1, nchan):
        pl.semaphore_signal(barrier, inc=1, device_id={"chan": chan_at(step)}, device_id_type=MESH)
    for step in range(1, nlon):
        pl.semaphore_signal(barrier, inc=1, device_id={"lon": lon_at(step)}, device_id_type=MESH)

    @pl.when(has_up)
    def _():
        for step in range(nchan):
            pl.semaphore_signal(
                barrier, inc=1, device_id={"lat": lat - 1, "chan": chan_at(step)}, device_id_type=MESH
            )

    @pl.when(has_down)
    def _():
        for step in range(nchan):
            pl.semaphore_signal(
                barrier, inc=1, device_id={"lat": lat + 1, "chan": chan_at(step)}, device_id_type=MESH
            )

    gap = (
        lax.broadcasted_iota(jnp.int32, (cols, wide), 1)
        - lax.broadcasted_iota(jnp.int32, (cols, wide), 0)
        - (EDGE - 1)
    )
    masks = [jnp.where(gap == t, 1.0, 0.0).astype(F32) for t in range(3)]
    def build_band(which):
        for i in range(rows):
            for k in range(KB):
                for e in range(3):
                    if which == 0:
                        c = [tab[i + 1, e * 9 + k * 3 + t] for t in range(3)]
                    else:
                        c = [tab[i + e, (2 - e) * 9 + k * 3 + 2 - t] for t in range(3)]
                    block = masks[0] * c[0] + masks[1] * c[1] + masks[2] * c[2]
                    band[which, i, k * cols:(k + 1) * cols, e * wide:(e + 1) * wide] = block.astype(BF16)

    sides = jnp.minimum(lat, 1) + jnp.minimum(nlat - 1 - lat, 1)
    pl.semaphore_wait(barrier, nchan + nlon - 2 + nchan * sides)

    def remote(src, dst, send, recv, where):
        return pltpu.make_async_remote_copy(
            src_ref=src, dst_ref=dst, send_sem=send, recv_sem=recv,
            device_id=where, device_id_type=MESH,
        )

    def block_copy(x, step, slot):
        return remote(
            ext.at[x, slot, 1:rows + 1, mid], ext.at[x, slot, 1:rows + 1, mid],
            x_send.at[x, step], x_recv.at[x, step], {"chan": chan_at(step)},
        )

    def row_copy(x, step, slot, down):
        src, dst = (rows, 0) if down else (1, rows + 1)
        sem = (2 if down else 1) * nchan + step
        return remote(
            ext.at[x, slot, pl.ds(src, 1), mid], ext.at[x, slot, pl.ds(dst, 1), mid],
            x_send.at[x, sem], x_recv.at[x, sem],
            {"lat": lat + 1 if down else lat - 1, "chan": chan_at(step)},
        )

    def col_copy(x, right):
        src, dst = (cols, 0) if right else (EDGE, EDGE + cols)
        sem = 3 * nchan + (1 if right else 0)
        return remote(
            ext.at[x, :, :, pl.ds(src, EDGE)], ext.at[x, :, :, pl.ds(dst, EDGE)],
            x_send.at[x, sem], x_recv.at[x, sem], {"lon": lon_at(1 if right else -1)},
        )

    def on_rows(x, what, own):
        @pl.when(has_down)
        def _():
            for step in range(nchan):
                if own:
                    what(row_copy(x, step, chan, True))
                else:
                    what(row_copy(x, step, chan_at(-step), False))

        @pl.when(has_up)
        def _():
            for step in range(nchan):
                if own:
                    what(row_copy(x, step, chan, False))
                else:
                    what(row_copy(x, step, chan_at(-step), True))

    def start_exchange(x):
        on_rows(x, lambda c: c.start(), True)
        for step in range(1, nchan):
            block_copy(x, step, chan).start()

    def wait_row(x, step, slot, down):
        dst = 0 if down else rows + 1
        sem = (2 if down else 1) * nchan + step
        remote(
            ext.at[x, slot, pl.ds(dst, 1), mid], ext.at[x, slot, pl.ds(dst, 1), mid],
            x_send.at[x, sem], x_recv.at[x, sem],
            {"lat": lat - 1 if down else lat + 1, "chan": chan_at(-step)},
        ).wait_recv()

    def finish_exchange(x):
        @pl.when(has_up)
        def _():
            for step in range(nchan):
                wait_row(x, step, chan_at(-step), True)

        @pl.when(has_down)
        def _():
            for step in range(nchan):
                wait_row(x, step, chan_at(-step), False)

        for step in range(1, nchan):
            block_copy(x, step, chan_at(-step)).wait_recv()
        col_copy(x, True).start()
        col_copy(x, False).start()
        col_copy(x, True).wait_recv()
        col_copy(x, False).wait_recv()

    def end_exchange(x):
        on_rows(x, lambda c: c.wait_send(), True)
        for step in range(1, nchan):
            block_copy(x, step, chan).wait_send()
        col_copy(x, True).wait_send()
        col_copy(x, False).wait_send()

    half_w = width // nlon
    weights = (w1, w2)

    def weight_copy(which, step, peer, slot):
        return remote(
            weights[which].at[:, pl.ds(pl.multiple_of(peer * width + lon * half_w, half_w), half_w)],
            wb.at[which, :, pl.ds(pl.multiple_of(lon * half_w, half_w), half_w),
                  pl.ds(pl.multiple_of(slot * width, width), width)],
            w_send.at[which, step], w_recv.at[which, step], {"chan": chan_at(step)},
        )

    def forward_copy(which, step, hop, owner):
        at = (
            which, slice(None), pl.ds(pl.multiple_of(owner * half_w, half_w), half_w),
            pl.ds(pl.multiple_of(chan_at(-step) * width, width), width),
        )
        return remote(
            wb.at[at], wb.at[at], f_send.at[which, step, hop], f_recv.at[which, step, hop],
            {"lon": lon_at(hop)},
        )

    def apply_filter(which, x, out):
        for i in range(rows):
            for slot in range(nchan):
                seen = ext[x, slot, i:i + 3].reshape(3 * wide, width)
                got = jnp.dot(band[which, i], seen, preferred_element_type=F32).astype(BF16)
                for k in range(KB):
                    out[i * cols:(i + 1) * cols,
                        k * channels + slot * width:k * channels + (slot + 1) * width] = got[
                            k * cols:(k + 1) * cols]

    def put(x, value):
        ext[x, chan, 1:rows + 1, mid] = value.reshape(rows, cols, width)

    def mix_back(which):
        total = None
        for k in range(KB):
            term = lax.dot_general(
                vb[:, k * channels:(k + 1) * channels], wb[which, k],
                (((1,), (1,)), ((), ())), preferred_element_type=F32,
            )
            total = term if total is None else total + term
        return total

    full_rows = KB * channels
    share = full_rows // nlon
    piece = share // chunks

    def rs_copy(g, step):
        return remote(
            rs_out.at[g, step - 1], rs_in.at[g, step - 1], rs_send.at[g, step - 1],
            rs_recv.at[g, step - 1], {"lon": lon_at(step)},
        )

    def weight_gradient(g, v, dpre):
        for k in range(KB):
            part[g, k * channels:(k + 1) * channels] = lax.dot_general(
                v[:, k * channels:(k + 1) * channels], dpre,
                (((0,), (0,)), ((), ())), preferred_element_type=F32,
            )
        for step in range(1, nlon):
            rs_out[g, step - 1] = part[
                g, pl.ds(pl.multiple_of(lon_at(step) * share, share), share)].astype(BF16)
            rs_copy(g, step).start()

    def chain_copy(g, j, right):
        out, into = (s_right, r_right) if right else (s_left, r_left)
        side = 0 if right else 1
        return remote(
            out.at[g, j], into.at[g, j], c_send.at[g, side, j], c_recv.at[g, side, j],
            {"lat": lat + 1 if right else lat - 1},
        )

    def chain_wait(g, j, right):
        into = r_right if right else r_left
        side = 0 if right else 1
        remote(
            into.at[g, j], into.at[g, j], c_send.at[g, side, j], c_recv.at[g, side, j],
            {"lat": lat - 1 if right else lat + 1},
        ).wait_recv()

    def ag_copy(g, j, step):
        return remote(
            ag_out.at[g, j], ag_in.at[g, step - 1, j], ag_send.at[g, step - 1, j],
            ag_recv.at[g, step - 1, j], {"lon": lon_at(step)},
        )

    def chain(g, out):
        for step in range(1, nlon):
            rs_copy(g, step).wait_recv()
        own = part[g, pl.ds(pl.multiple_of(lon * share, share), share)]
        for step in range(1, nlon):
            own = own + rs_in[g, step - 1].astype(F32)
        tot[g] = own.reshape(chunks, piece, width)
        rest = nlat - 1 - lat
        late = jnp.maximum(lat, rest)

        def tick(time, carry):
            j_right = time - lat
            j_left = time - rest
            j_done = time - late

            @pl.when((j_right >= 0) & (j_right < chunks) & (lat == 0))
            def _():
                s_right[g, j_right] = tot[g, j_right].astype(BF16)

            @pl.when((j_right >= 0) & (j_right < chunks) & (lat > 0))
            def _():
                chain_wait(g, j_right, True)
                s_right[g, j_right] = (tot[g, j_right] + r_right[g, j_right].astype(F32)).astype(BF16)

            @pl.when((j_right >= 0) & (j_right < chunks) & has_down)
            def _():
                chain_copy(g, j_right, True).start()

            @pl.when((j_left >= 0) & (j_left < chunks) & (rest == 0))
            def _():
                s_left[g, j_left] = tot[g, j_left].astype(BF16)

            @pl.when((j_left >= 0) & (j_left < chunks) & (rest > 0))
            def _():
                chain_wait(g, j_left, False)
                s_left[g, j_left] = (tot[g, j_left] + r_left[g, j_left].astype(F32)).astype(BF16)

            @pl.when((j_left >= 0) & (j_left < chunks) & has_up)
            def _():
                chain_copy(g, j_left, False).start()

            @pl.when((j_done >= 0) & (j_done < chunks))
            def _():
                @pl.when(has_up)
                def _():
                    tot[g, j_done] = tot[g, j_done] + r_right[g, j_done].astype(F32)

                @pl.when(has_down)
                def _():
                    tot[g, j_done] = tot[g, j_done] + r_left[g, j_done].astype(F32)

                ag_out[g, j_done] = tot[g, j_done].astype(BF16)
                for step in range(1, nlon):
                    ag_copy(g, j_done, step).start()

            return carry

        lax.fori_loop(0, nlat - 1 + chunks, tick, 0)
        out[pl.ds(pl.multiple_of(lon * share, share), share)] = tot[g].reshape(share, width)

    def chain_end(g, out):
        def settle(j, carry):
            for step in range(1, nlon):
                ag_copy(g, j, step).wait_recv()
                ag_copy(g, j, step).wait_send()

            @pl.when(has_down)
            def _():
                chain_copy(g, j, True).wait_send()

            @pl.when(has_up)
            def _():
                chain_copy(g, j, False).wait_send()

            return carry

        lax.fori_loop(0, chunks, settle, 0)
        for step in range(1, nlon):
            out[pl.ds(pl.multiple_of(lon_at(-step) * share, share), share)] = (
                ag_in[g, step - 1].reshape(share, width).astype(F32)
            )
            rs_copy(g, step).wait_send()

    put(0, act[...])
    start_exchange(0)
    for which in (1, 0):
        for step in range(1, nchan):
            weight_copy(which, step, chan_at(step), chan).start()
    build_band(0)
    build_band(1)
    for which in (1, 0):
        wb[which, :, :, pl.ds(pl.multiple_of(chan * width, width), width)] = weights[which][
            :, pl.ds(pl.multiple_of(chan * width, width), width)]
    finish_exchange(0)
    apply_filter(0, 0, v1)
    first = jnp.dot(v1[...], w1[...].reshape(full_rows, width), preferred_element_type=F32)
    pre1[...] = first
    hidden = (act[...].reshape(rows * cols, width).astype(F32) + gelu(first)).astype(BF16)
    put(1, hidden)
    start_exchange(1)
    for which in (1, 0):
        for step in range(1, nchan):
            weight_copy(which, step, chan, chan_at(-step)).wait_recv()
            for hop in range(1, nlon):
                forward_copy(which, step, hop, lon).start()
    finish_exchange(1)
    apply_filter(0, 1, v2)
    second = jnp.dot(v2[...], w2[...].reshape(full_rows, width), preferred_element_type=F32)
    upstream = cot[...].reshape(rows * cols, width).astype(F32)
    dpre2 = (upstream * gelu_slope(second)).astype(BF16)
    put(2, dpre2)
    start_exchange(2)
    held = ext[1, chan, 1:rows + 1, mid].reshape(rows * cols, width).astype(F32)
    mixed[...] = (held + gelu(second)).astype(BF16).reshape(rows, cols, width)
    weight_gradient(0, v2, dpre2)
    for which in (1, 0):
        for step in range(1, nchan):
            for hop in range(1, nlon):
                forward_copy(which, step, hop, lon_at(-hop)).wait_recv()
    finish_exchange(2)
    apply_filter(1, 2, vb)
    back_hidden = (cot[...].reshape(rows * cols, width).astype(F32) + mix_back(1)).astype(BF16)
    back[...] = back_hidden
    dpre1 = (back_hidden.astype(F32) * gelu_slope(pre1[...])).astype(BF16)
    put(3, dpre1)
    start_exchange(3)
    weight_gradient(1, v1, dpre1)
    chain(0, g2)
    finish_exchange(3)
    apply_filter(1, 3, vb)
    gin[...] = (back[...].astype(F32) + mix_back(0)).reshape(rows, cols, width)
    chain(1, g1)
    chain_end(0, g2)
    chain_end(1, g1)
    for x in range(4):
        end_exchange(x)
    for which in (1, 0):
        for step in range(1, nchan):
            weight_copy(which, step, chan_at(step), chan).wait_send()
            for hop in range(1, nlon):
                forward_copy(which, step, hop, lon).wait_send()


def body(sizes, activations, cotangent, w_first, w_second, offsets, basis, live, taps):
    nlat, nchan, nlon, chunks = sizes
    rows, cols, width = activations.shape
    channels = w_first.shape[1]
    wide = cols + 2 * EDGE
    table = coefficients(offsets, basis, live, taps).reshape(offsets.shape[0], 9 * KB)
    table = jnp.pad(table, ((HALO, HALO), (0, 0)))
    near = lax.dynamic_slice_in_dim(table, lax.axis_index("lat") * rows, rows + 2 * HALO, 0)
    full_rows = KB * channels
    share = full_rows // nlon
    piece = share // chunks
    cells = rows * cols
    dma = pltpu.SemaphoreType.DMA
    vmem = pl.BlockSpec(memory_space=pltpu.VMEM)
    slots = 3 * nchan + 2
    mixed, gin, g1, g2 = pl.pallas_call(
        functools.partial(kernel, sizes),
        out_shape=(
            jax.ShapeDtypeStruct((rows, cols, width), BF16),
            jax.ShapeDtypeStruct((rows, cols, width), F32),
            jax.ShapeDtypeStruct((full_rows, width), F32),
            jax.ShapeDtypeStruct((full_rows, width), F32),
        ),
        in_specs=[pl.BlockSpec(memory_space=pltpu.SMEM)] + [vmem] * 4,
        out_specs=(vmem,) * 4,
        scratch_shapes=[
            pltpu.VMEM((4, nchan, rows + 2, wide, width), BF16),
            pltpu.VMEM((2, KB, width, channels), BF16),
            pltpu.VMEM((2, rows, KB * cols, 3 * wide), BF16),
            pltpu.VMEM((cells, full_rows), BF16),
            pltpu.VMEM((cells, full_rows), BF16),
            pltpu.VMEM((cells, full_rows), BF16),
            pltpu.VMEM((cells, width), F32),
            pltpu.VMEM((cells, width), BF16),
            pltpu.VMEM((2, full_rows, width), F32),
            pltpu.VMEM((2, nlon - 1, share, width), BF16),
            pltpu.VMEM((2, nlon - 1, share, width), BF16),
            pltpu.VMEM((2, chunks, piece, width), F32),
            pltpu.VMEM((2, chunks, piece, width), BF16),
            pltpu.VMEM((2, chunks, piece, width), BF16),
            pltpu.VMEM((2, chunks, piece, width), BF16),
            pltpu.VMEM((2, chunks, piece, width), BF16),
            pltpu.VMEM((2, chunks, piece, width), BF16),
            pltpu.VMEM((2, nlon - 1, chunks, piece, width), BF16),
            dma((4, slots)),
            dma((4, slots)),
            dma((2, nchan)),
            dma((2, nchan)),
            dma((2, nchan, nlon)),
            dma((2, nchan, nlon)),
            dma((2, nlon - 1)),
            dma((2, nlon - 1)),
            dma((2, 2, chunks)),
            dma((2, 2, chunks)),
            dma((2, nlon - 1, chunks)),
            dma((2, nlon - 1, chunks)),
        ],
        compiler_params=pltpu.CompilerParams(
            collective_id=0, has_side_effects=True, vmem_limit_bytes=50 * 1024 * 1024
        ),
    )(near, activations, cotangent, w_first, w_second)
    shape = (KB, channels, width)
    return mixed, gin, g1.reshape(shape), g2.reshape(shape)


def solution(mesh):
    sizes = (mesh.shape["lat"], mesh.shape["chan"], mesh.shape["lon"], 8)
    return jax.shard_map(
        functools.partial(body, sizes),
        mesh=mesh,
        in_specs=(
            P(("groups", "lat"), "lon", "chan"),
            P(("groups", "lat"), "lon", "chan"),
            P(None, None, "chan"),
            P(None, None, "chan"),
            P(),
            P(),
            P(),
            P(),
        ),
        out_specs=(
            P(("groups", "lat"), "lon", "chan"),
            P(("groups", "lat"), "lon", "chan"),
            P("groups", None, "chan"),
            P("groups", None, "chan"),
        ),
        check_vma=False,
    )
```

```python
import functools
import math

import jax
import jax.numpy as jnp
from jax import lax
from jax.experimental import pallas as pl
from jax.experimental.pallas import tpu as pltpu
from jax.sharding import PartitionSpec as P

KB = 3
HALO = 1
EDGE = 16
MESH = pl.DeviceIdType.MESH
BF16 = jnp.bfloat16
F32 = jnp.float32
GELU_C = math.sqrt(2.0 / math.pi)
GELU_A = 0.044715


def coefficients(offsets, basis, live, taps):
    stencil = 2 * HALO + 1
    slot_count = offsets.shape[1]
    in_use = jnp.arange(slot_count)[None, :] < live[:, None]
    row_hit = (offsets[:, :, None] == (jnp.arange(stencil) - HALO)[None, None, :]) & in_use[
        :, :, None
    ]
    kind_hit = basis[:, :, None] == jnp.arange(KB)[None, None, :]
    chosen = row_hit[:, :, :, None] & kind_hit[:, :, None, :]
    return jnp.sum(
        jnp.where(chosen[..., None], taps[:, :, None, None, :], jnp.float32(0.0)), axis=1
    )


def gelu(x):
    th = jnp.tanh(GELU_C * (x + GELU_A * (x * x * x)))
    return 0.5 * x * (1.0 + th)


def gelu_slope(x):
    sq = x * x
    th = jnp.tanh(GELU_C * (x + GELU_A * (sq * x)))
    return 0.5 * (1.0 + th) + (0.5 * x) * (1.0 - th * th) * (
        GELU_C * (1.0 + (3.0 * GELU_A) * sq)
    )


def kernel(
    sizes, tab, act_in, cot_in, w1_in, w2_in, mixed, gin, g1, g2,
    act, cot, w1, w2, ext, wb, band, v1, v2, vb, pre1, back, part, rs_out, rs_in, tot,
    s_right, r_right, s_left, r_left, ag_out, ag_in,
    x_send, x_recv, w_send, w_recv, f_send, f_recv, rs_send, rs_recv, c_send, c_recv,
    ag_send, ag_recv, in_sem,
):
    nlat, nchan, nlon, chunks = sizes
    first_ticks, mid_ticks = chunks - 1, chunks
    rows, cols, width = act_in.shape
    channels = nchan * width
    wide = cols + 2 * EDGE
    lat, chan, lon = lax.axis_index("lat"), lax.axis_index("chan"), lax.axis_index("lon")
    has_up, has_down = lat > 0, lat < nlat - 1
    loads = [
        pltpu.make_async_copy(src, dst, in_sem.at[n])
        for n, (src, dst) in enumerate(((act_in, act), (w1_in, w1), (w2_in, w2), (cot_in, cot)))
    ]
    for load in loads:
        load.start()
    mid = pl.ds(EDGE, cols)

    @pl.when(lat == 0)
    def _():
        ext[:, :, 0] = jnp.zeros(ext.shape[:2] + ext.shape[3:], BF16)

    @pl.when(lat == nlat - 1)
    def _():
        ext[:, :, rows + 1] = jnp.zeros(ext.shape[:2] + ext.shape[3:], BF16)

    barrier = pltpu.get_barrier_semaphore()

    def chan_at(step):
        return lax.rem(chan + step + nchan, nchan)

    def lon_at(step):
        return lax.rem(lon + step + nlon, nlon)

    for step in range(1, nchan):
        pl.semaphore_signal(barrier, inc=1, device_id={"chan": chan_at(step)}, device_id_type=MESH)
    for step in range(1, nlon):
        pl.semaphore_signal(barrier, inc=1, device_id={"lon": lon_at(step)}, device_id_type=MESH)

    @pl.when(has_up)
    def _():
        for step in range(nchan):
            pl.semaphore_signal(
                barrier, inc=1, device_id={"lat": lat - 1, "chan": chan_at(step)}, device_id_type=MESH
            )

    @pl.when(has_down)
    def _():
        for step in range(nchan):
            pl.semaphore_signal(
                barrier, inc=1, device_id={"lat": lat + 1, "chan": chan_at(step)}, device_id_type=MESH
            )

    gap = (
        lax.broadcasted_iota(jnp.int32, (cols, wide), 1)
        - lax.broadcasted_iota(jnp.int32, (cols, wide), 0)
        - (EDGE - 1)
    )
    masks = [jnp.where(gap == t, 1.0, 0.0).astype(F32) for t in range(3)]
    def build_band(which):
        for i in range(rows):
            for k in range(KB):
                for e in range(3):
                    if which == 0:
                        c = [tab[i + 1, e * 9 + k * 3 + t] for t in range(3)]
                    else:
                        c = [tab[i + e, (2 - e) * 9 + k * 3 + 2 - t] for t in range(3)]
                    block = masks[0] * c[0] + masks[1] * c[1] + masks[2] * c[2]
                    band[which, i, k * cols:(k + 1) * cols, e * wide:(e + 1) * wide] = block.astype(BF16)

    sides = jnp.minimum(lat, 1) + jnp.minimum(nlat - 1 - lat, 1)
    pl.semaphore_wait(barrier, nchan + nlon - 2 + nchan * sides)

    def remote(src, dst, send, recv, where):
        return pltpu.make_async_remote_copy(
            src_ref=src, dst_ref=dst, send_sem=send, recv_sem=recv,
            device_id=where, device_id_type=MESH,
        )

    def block_copy(x, step, slot):
        return remote(
            ext.at[x, slot, 1:rows + 1, mid], ext.at[x, slot, 1:rows + 1, mid],
            x_send.at[x, step], x_recv.at[x, step], {"chan": chan_at(step)},
        )

    def row_copy(x, step, slot, down):
        src, dst = (rows, 0) if down else (1, rows + 1)
        sem = (2 if down else 1) * nchan + step
        return remote(
            ext.at[x, slot, pl.ds(src, 1), mid], ext.at[x, slot, pl.ds(dst, 1), mid],
            x_send.at[x, sem], x_recv.at[x, sem],
            {"lat": lat + 1 if down else lat - 1, "chan": chan_at(step)},
        )

    def col_copy(x, right):
        src, dst = (cols, 0) if right else (EDGE, EDGE + cols)
        sem = 3 * nchan + (1 if right else 0)
        return remote(
            ext.at[x, :, :, pl.ds(src, EDGE)], ext.at[x, :, :, pl.ds(dst, EDGE)],
            x_send.at[x, sem], x_recv.at[x, sem], {"lon": lon_at(1 if right else -1)},
        )

    def on_rows(x, what, own):
        @pl.when(has_down)
        def _():
            for step in range(nchan):
                if own:
                    what(row_copy(x, step, chan, True))
                else:
                    what(row_copy(x, step, chan_at(-step), False))

        @pl.when(has_up)
        def _():
            for step in range(nchan):
                if own:
                    what(row_copy(x, step, chan, False))
                else:
                    what(row_copy(x, step, chan_at(-step), True))

    def start_exchange(x):
        on_rows(x, lambda c: c.start(), True)
        for step in range(1, nchan):
            block_copy(x, step, chan).start()

    def wait_row(x, step, slot, down):
        dst = 0 if down else rows + 1
        sem = (2 if down else 1) * nchan + step
        remote(
            ext.at[x, slot, pl.ds(dst, 1), mid], ext.at[x, slot, pl.ds(dst, 1), mid],
            x_send.at[x, sem], x_recv.at[x, sem],
            {"lat": lat - 1 if down else lat + 1, "chan": chan_at(-step)},
        ).wait_recv()

    def finish_middle(x):
        @pl.when(has_up)
        def _():
            for step in range(nchan):
                wait_row(x, step, chan_at(-step), True)

        @pl.when(has_down)
        def _():
            for step in range(nchan):
                wait_row(x, step, chan_at(-step), False)

        for step in range(1, nchan):
            block_copy(x, step, chan_at(-step)).wait_recv()
        col_copy(x, True).start()
        col_copy(x, False).start()

    def finish_columns(x):
        col_copy(x, True).wait_recv()
        col_copy(x, False).wait_recv()

    def finish_exchange(x):
        finish_middle(x)
        finish_columns(x)

    def end_exchange(x):
        on_rows(x, lambda c: c.wait_send(), True)
        for step in range(1, nchan):
            block_copy(x, step, chan).wait_send()
        col_copy(x, True).wait_send()
        col_copy(x, False).wait_send()

    half_w = width // nlon
    weights = (w1, w2)

    def weight_copy(which, step, peer, slot):
        return remote(
            weights[which].at[:, pl.ds(pl.multiple_of(peer * width + lon * half_w, half_w), half_w)],
            wb.at[which, :, pl.ds(pl.multiple_of(lon * half_w, half_w), half_w),
                  pl.ds(pl.multiple_of(slot * width, width), width)],
            w_send.at[which, step], w_recv.at[which, step], {"chan": chan_at(step)},
        )

    def forward_copy(which, step, hop, owner):
        at = (
            which, slice(None), pl.ds(pl.multiple_of(owner * half_w, half_w), half_w),
            pl.ds(pl.multiple_of(chan_at(-step) * width, width), width),
        )
        return remote(
            wb.at[at], wb.at[at], f_send.at[which, step, hop], f_recv.at[which, step, hop],
            {"lon": lon_at(hop)},
        )

    def apply_filter(which, x, out):
        for i in range(rows):
            for slot in range(nchan):
                seen = ext[x, slot, i:i + 3].reshape(3 * wide, width)
                got = jnp.dot(band[which, i], seen, preferred_element_type=F32).astype(BF16)
                for k in range(KB):
                    out[i * cols:(i + 1) * cols,
                        k * channels + slot * width:k * channels + (slot + 1) * width] = got[
                            k * cols:(k + 1) * cols]

    def put(x, value):
        ext[x, chan, 1:rows + 1, mid] = value.reshape(rows, cols, width)

    def mix_back(which):
        total = None
        for k in range(KB):
            term = lax.dot_general(
                vb[:, k * channels:(k + 1) * channels], wb[which, k],
                (((1,), (1,)), ((), ())), preferred_element_type=F32,
            )
            total = term if total is None else total + term
        return total

    full_rows = KB * channels
    share = full_rows // nlon
    piece = share // chunks

    def rs_copy(g, step):
        return remote(
            rs_out.at[g, step - 1], rs_in.at[g, step - 1], rs_send.at[g, step - 1],
            rs_recv.at[g, step - 1], {"lon": lon_at(step)},
        )

    def weight_gradient(g, v, dpre):
        for k in range(KB):
            part[g, k * channels:(k + 1) * channels] = lax.dot_general(
                v[:, k * channels:(k + 1) * channels], dpre,
                (((0,), (0,)), ((), ())), preferred_element_type=F32,
            )
        for step in range(1, nlon):
            rs_out[g, step - 1] = part[
                g, pl.ds(pl.multiple_of(lon_at(step) * share, share), share)].astype(BF16)
            rs_copy(g, step).start()

    def chain_copy(j, right):
        out, into = (s_right, r_right) if right else (s_left, r_left)
        side = 0 if right else 1
        return remote(
            out.at[j], into.at[j], c_send.at[side, j], c_recv.at[side, j],
            {"lat": lat + 1 if right else lat - 1},
        )

    def chain_wait(j, right):
        into = r_right if right else r_left
        side = 0 if right else 1
        remote(
            into.at[j], into.at[j], c_send.at[side, j], c_recv.at[side, j],
            {"lat": lat - 1 if right else lat + 1},
        ).wait_recv()

    def ag_copy(j, step):
        return remote(
            ag_out.at[j], ag_in.at[step - 1, j], ag_send.at[step - 1, j],
            ag_recv.at[step - 1, j], {"lon": lon_at(step)},
        )

    def prepare(g):
        for step in range(1, nlon):
            rs_copy(g, step).wait_recv()
        own = part[g, pl.ds(pl.multiple_of(lon * share, share), share)]
        for step in range(1, nlon):
            own = own + rs_in[g, step - 1].astype(F32)
        tot[g * chunks:(g + 1) * chunks] = own.reshape(chunks, piece, width)

    rest = nlat - 1 - lat
    late = jnp.maximum(lat, rest)
    both = 2 * chunks

    def tick(time, carry):
        j_right = time - lat
        j_left = time - rest
        j_done = time - late
        do_right = (j_right >= 0) & (j_right < both)
        do_left = (j_left >= 0) & (j_left < both)

        @pl.when(do_right & (lat == 0))
        def _():
            s_right[j_right] = tot[j_right].astype(BF16)

        @pl.when(do_right & (lat > 0))
        def _():
            chain_wait(j_right, True)
            s_right[j_right] = (tot[j_right] + r_right[j_right].astype(F32)).astype(BF16)

        @pl.when(do_right & has_down)
        def _():
            chain_copy(j_right, True).start()

        @pl.when(do_left & (rest == 0))
        def _():
            s_left[j_left] = tot[j_left].astype(BF16)

        @pl.when(do_left & (rest > 0))
        def _():
            chain_wait(j_left, False)
            s_left[j_left] = (tot[j_left] + r_left[j_left].astype(F32)).astype(BF16)

        @pl.when(do_left & has_up)
        def _():
            chain_copy(j_left, False).start()

        @pl.when((j_done >= 0) & (j_done < both))
        def _():
            @pl.when(has_up)
            def _():
                tot[j_done] = tot[j_done] + r_right[j_done].astype(F32)

            @pl.when(has_down)
            def _():
                tot[j_done] = tot[j_done] + r_left[j_done].astype(F32)

            ag_out[j_done] = tot[j_done].astype(BF16)
            for step in range(1, nlon):
                ag_copy(j_done, step).start()

        return carry

    def settle():
        def one(j, carry):
            for step in range(1, nlon):
                ag_copy(j, step).wait_recv()
                ag_copy(j, step).wait_send()

            @pl.when(has_down)
            def _():
                chain_copy(j, True).wait_send()

            @pl.when(has_up)
            def _():
                chain_copy(j, False).wait_send()

            return carry

        lax.fori_loop(0, both, one, 0)
        for g, out in ((0, g2), (1, g1)):
            span = slice(g * chunks, (g + 1) * chunks)
            out[pl.ds(pl.multiple_of(lon * share, share), share)] = ag_out[span].reshape(share, width)
            for step in range(1, nlon):
                out[pl.ds(pl.multiple_of(lon_at(-step) * share, share), share)] = (
                    ag_in[step - 1, span].reshape(share, width)
                )
                rs_copy(g, step).wait_send()

    loads[0].wait()
    put(0, act[...])
    start_exchange(0)
    for load in loads[1:]:
        load.wait()
    for which in (1, 0):
        for step in range(1, nchan):
            weight_copy(which, step, chan_at(step), chan).start()
    build_band(0)
    build_band(1)
    for which in (1, 0):
        wb[which, :, :, pl.ds(pl.multiple_of(chan * width, width), width)] = weights[which][
            :, pl.ds(pl.multiple_of(chan * width, width), width)]
    finish_exchange(0)
    apply_filter(0, 0, v1)
    first = jnp.dot(v1[...], w1[...].reshape(full_rows, width), preferred_element_type=F32)
    pre1[...] = first
    hidden = (act[...].reshape(rows * cols, width).astype(F32) + gelu(first)).astype(BF16)
    put(1, hidden)
    start_exchange(1)
    for which in (1, 0):
        for step in range(1, nchan):
            weight_copy(which, step, chan, chan_at(-step)).wait_recv()
            for hop in range(1, nlon):
                forward_copy(which, step, hop, lon).start()
    finish_exchange(1)
    apply_filter(0, 1, v2)
    second = jnp.dot(v2[...], w2[...].reshape(full_rows, width), preferred_element_type=F32)
    upstream = cot[...].reshape(rows * cols, width).astype(F32)
    dpre2 = (upstream * gelu_slope(second)).astype(BF16)
    put(2, dpre2)
    start_exchange(2)
    held = ext[1, chan, 1:rows + 1, mid].reshape(rows * cols, width).astype(F32)
    mixed[...] = (held + gelu(second)).astype(BF16).reshape(rows, cols, width)
    weight_gradient(0, v2, dpre2)
    for which in (1, 0):
        for step in range(1, nchan):
            for hop in range(1, nlon):
                forward_copy(which, step, hop, lon_at(-hop)).wait_recv()
    prepare(0)
    lax.fori_loop(0, first_ticks, tick, 0)
    finish_exchange(2)
    apply_filter(1, 2, vb)
    back_hidden = (cot[...].reshape(rows * cols, width).astype(F32) + mix_back(1)).astype(BF16)
    back[...] = back_hidden
    dpre1 = (back_hidden.astype(F32) * gelu_slope(pre1[...])).astype(BF16)
    put(3, dpre1)
    start_exchange(3)
    weight_gradient(1, v1, dpre1)
    lax.fori_loop(first_ticks, chunks, tick, 0)
    prepare(1)
    lax.fori_loop(chunks, chunks + mid_ticks, tick, 0)
    finish_middle(3)
    lax.fori_loop(chunks + mid_ticks, nlat - 1 + both, tick, 0)
    finish_columns(3)
    apply_filter(1, 3, vb)
    gin[...] = (back[...].astype(F32) + mix_back(0)).reshape(rows, cols, width)
    settle()
    for x in range(4):
        end_exchange(x)
    for which in (1, 0):
        for step in range(1, nchan):
            weight_copy(which, step, chan_at(step), chan).wait_send()
            for hop in range(1, nlon):
                forward_copy(which, step, hop, lon).wait_send()


def body(sizes, activations, cotangent, w_first, w_second, offsets, basis, live, taps):
    nlat, nchan, nlon, chunks = sizes
    rows, cols, width = activations.shape
    channels = w_first.shape[1]
    wide = cols + 2 * EDGE
    table = coefficients(offsets, basis, live, taps).reshape(offsets.shape[0], 9 * KB)
    table = jnp.pad(table, ((HALO, HALO), (0, 0)))
    near = lax.dynamic_slice_in_dim(table, lax.axis_index("lat") * rows, rows + 2 * HALO, 0)
    full_rows = KB * channels
    share = full_rows // nlon
    piece = share // chunks
    cells = rows * cols
    dma = pltpu.SemaphoreType.DMA
    vmem = pl.BlockSpec(memory_space=pltpu.VMEM)
    slots = 3 * nchan + 2
    mixed, gin, g1, g2 = pl.pallas_call(
        functools.partial(kernel, sizes),
        out_shape=(
            jax.ShapeDtypeStruct((rows, cols, width), BF16),
            jax.ShapeDtypeStruct((rows, cols, width), F32),
            jax.ShapeDtypeStruct((full_rows, width), BF16),
            jax.ShapeDtypeStruct((full_rows, width), BF16),
        ),
        in_specs=[pl.BlockSpec(memory_space=pltpu.SMEM)] + [pl.BlockSpec(memory_space=pltpu.HBM)] * 4,
        out_specs=(vmem,) * 4,
        scratch_shapes=[
            pltpu.VMEM((rows, cols, width), BF16),
            pltpu.VMEM((rows, cols, width), BF16),
            pltpu.VMEM((KB, channels, width), BF16),
            pltpu.VMEM((KB, channels, width), BF16),
            pltpu.VMEM((4, nchan, rows + 2, wide, width), BF16),
            pltpu.VMEM((2, KB, width, channels), BF16),
            pltpu.VMEM((2, rows, KB * cols, 3 * wide), BF16),
            pltpu.VMEM((cells, full_rows), BF16),
            pltpu.VMEM((cells, full_rows), BF16),
            pltpu.VMEM((cells, full_rows), BF16),
            pltpu.VMEM((cells, width), F32),
            pltpu.VMEM((cells, width), BF16),
            pltpu.VMEM((2, full_rows, width), F32),
            pltpu.VMEM((2, nlon - 1, share, width), BF16),
            pltpu.VMEM((2, nlon - 1, share, width), BF16),
            pltpu.VMEM((2 * chunks, piece, width), F32),
            pltpu.VMEM((2 * chunks, piece, width), BF16),
            pltpu.VMEM((2 * chunks, piece, width), BF16),
            pltpu.VMEM((2 * chunks, piece, width), BF16),
            pltpu.VMEM((2 * chunks, piece, width), BF16),
            pltpu.VMEM((2 * chunks, piece, width), BF16),
            pltpu.VMEM((nlon - 1, 2 * chunks, piece, width), BF16),
            dma((4, slots)),
            dma((4, slots)),
            dma((2, nchan)),
            dma((2, nchan)),
            dma((2, nchan, nlon)),
            dma((2, nchan, nlon)),
            dma((2, nlon - 1)),
            dma((2, nlon - 1)),
            dma((2, 2 * chunks)),
            dma((2, 2 * chunks)),
            dma((nlon - 1, 2 * chunks)),
            dma((nlon - 1, 2 * chunks)),
            dma((4,)),
        ],
        compiler_params=pltpu.CompilerParams(
            collective_id=0, has_side_effects=True, vmem_limit_bytes=50 * 1024 * 1024
        ),
    )(near, activations, cotangent, w_first, w_second)
    shape = (KB, channels, width)
    return mixed, gin, g1.astype(F32).reshape(shape), g2.astype(F32).reshape(shape)


def solution(mesh):
    sizes = (mesh.shape["lat"], mesh.shape["chan"], mesh.shape["lon"], 3)
    return jax.shard_map(
        functools.partial(body, sizes),
        mesh=mesh,
        in_specs=(
            P(("groups", "lat"), "lon", "chan"),
            P(("groups", "lat"), "lon", "chan"),
            P(None, None, "chan"),
            P(None, None, "chan"),
            P(),
            P(),
            P(),
            P(),
        ),
        out_specs=(
            P(("groups", "lat"), "lon", "chan"),
            P(("groups", "lat"), "lon", "chan"),
            P("groups", None, "chan"),
            P("groups", None, "chan"),
        ),
        check_vma=False,
    )
```

```python
import functools
import math

import jax
import jax.numpy as jnp
from jax import lax
from jax.experimental import pallas as pl
from jax.experimental.pallas import tpu as pltpu
from jax.sharding import PartitionSpec as P

KB = 3
HALO = 1
EDGE = 16
MESH = pl.DeviceIdType.MESH
BF16 = jnp.bfloat16
F32 = jnp.float32
GELU_C = math.sqrt(2.0 / math.pi)
GELU_A = 0.044715


def coefficients(offsets, basis, live, taps):
    stencil = 2 * HALO + 1
    slot_count = offsets.shape[1]
    in_use = jnp.arange(slot_count)[None, :] < live[:, None]
    row_hit = (offsets[:, :, None] == (jnp.arange(stencil) - HALO)[None, None, :]) & in_use[
        :, :, None
    ]
    kind_hit = basis[:, :, None] == jnp.arange(KB)[None, None, :]
    chosen = row_hit[:, :, :, None] & kind_hit[:, :, None, :]
    return jnp.sum(
        jnp.where(chosen[..., None], taps[:, :, None, None, :], jnp.float32(0.0)), axis=1
    )


def gelu(x):
    th = jnp.tanh(GELU_C * (x + GELU_A * (x * x * x)))
    return 0.5 * x * (1.0 + th)


def gelu_slope(x):
    sq = x * x
    th = jnp.tanh(GELU_C * (x + GELU_A * (sq * x)))
    return 0.5 * (1.0 + th) + (0.5 * x) * (1.0 - th * th) * (
        GELU_C * (1.0 + (3.0 * GELU_A) * sq)
    )


def kernel(
    sizes, tab, act_in, cot_in, w1_in, w2_in, mixed, gin, g1, g2,
    act, cot, w1, w2, ext, wb, band, v1, v2, vb, pre1, back, part, rs_out, rs_in, tot,
    s_right, r_right, s_left, r_left, ag_out, ag_in,
    x_send, x_recv, w_send, w_recv, f_send, f_recv, rs_send, rs_recv, c_send, c_recv,
    ag_send, ag_recv, in_sem,
):
    nlat, nchan, nlon, chunks = sizes
    first_ticks, mid_ticks = chunks, chunks
    rows, cols, width = act_in.shape
    channels = nchan * width
    wide = cols + 2 * EDGE
    lat, chan, lon = lax.axis_index("lat"), lax.axis_index("chan"), lax.axis_index("lon")
    has_up, has_down = lat > 0, lat < nlat - 1
    loads = [
        pltpu.make_async_copy(src, dst, in_sem.at[n])
        for n, (src, dst) in enumerate(((act_in, act), (w1_in, w1), (w2_in, w2), (cot_in, cot)))
    ]
    for load in loads:
        load.start()
    mid = pl.ds(EDGE, cols)

    @pl.when(lat == 0)
    def _():
        ext[:, :, 0] = jnp.zeros(ext.shape[:2] + ext.shape[3:], BF16)

    @pl.when(lat == nlat - 1)
    def _():
        ext[:, :, rows + 1] = jnp.zeros(ext.shape[:2] + ext.shape[3:], BF16)

    barrier = pltpu.get_barrier_semaphore()

    def chan_at(step):
        return lax.rem(chan + step + nchan, nchan)

    def lon_at(step):
        return lax.rem(lon + step + nlon, nlon)

    for step in range(1, nchan):
        pl.semaphore_signal(barrier, inc=1, device_id={"chan": chan_at(step)}, device_id_type=MESH)
    for step in range(1, nlon):
        pl.semaphore_signal(barrier, inc=1, device_id={"lon": lon_at(step)}, device_id_type=MESH)

    @pl.when(has_up)
    def _():
        for step in range(nchan):
            pl.semaphore_signal(
                barrier, inc=1, device_id={"lat": lat - 1, "chan": chan_at(step)}, device_id_type=MESH
            )

    @pl.when(has_down)
    def _():
        for step in range(nchan):
            pl.semaphore_signal(
                barrier, inc=1, device_id={"lat": lat + 1, "chan": chan_at(step)}, device_id_type=MESH
            )

    gap = (
        lax.broadcasted_iota(jnp.int32, (cols, wide), 1)
        - lax.broadcasted_iota(jnp.int32, (cols, wide), 0)
        - (EDGE - 1)
    )
    masks = [jnp.where(gap == t, 1.0, 0.0).astype(F32) for t in range(3)]
    def build_band(which):
        for i in range(rows):
            for k in range(KB):
                for e in range(3):
                    if which == 0:
                        c = [tab[i + 1, e * 9 + k * 3 + t] for t in range(3)]
                    else:
                        c = [tab[i + e, (2 - e) * 9 + k * 3 + 2 - t] for t in range(3)]
                    block = masks[0] * c[0] + masks[1] * c[1] + masks[2] * c[2]
                    band[which, i, k * cols:(k + 1) * cols, e * wide:(e + 1) * wide] = block.astype(BF16)

    sides = jnp.minimum(lat, 1) + jnp.minimum(nlat - 1 - lat, 1)
    pl.semaphore_wait(barrier, nchan + nlon - 2 + nchan * sides)

    def remote(src, dst, send, recv, where):
        return pltpu.make_async_remote_copy(
            src_ref=src, dst_ref=dst, send_sem=send, recv_sem=recv,
            device_id=where, device_id_type=MESH,
        )

    def block_copy(x, step, slot):
        return remote(
            ext.at[x, slot, 1:rows + 1, mid], ext.at[x, slot, 1:rows + 1, mid],
            x_send.at[x, step], x_recv.at[x, step], {"chan": chan_at(step)},
        )

    def row_copy(x, step, slot, down):
        src, dst = (rows, 0) if down else (1, rows + 1)
        sem = (2 if down else 1) * nchan + step
        return remote(
            ext.at[x, slot, pl.ds(src, 1), mid], ext.at[x, slot, pl.ds(dst, 1), mid],
            x_send.at[x, sem], x_recv.at[x, sem],
            {"lat": lat + 1 if down else lat - 1, "chan": chan_at(step)},
        )

    def col_copy(x, right):
        src, dst = (cols, 0) if right else (EDGE, EDGE + cols)
        sem = 3 * nchan + (1 if right else 0)
        return remote(
            ext.at[x, :, :, pl.ds(src, EDGE)], ext.at[x, :, :, pl.ds(dst, EDGE)],
            x_send.at[x, sem], x_recv.at[x, sem], {"lon": lon_at(1 if right else -1)},
        )

    def on_rows(x, what, own):
        @pl.when(has_down)
        def _():
            for step in range(nchan):
                if own:
                    what(row_copy(x, step, chan, True))
                else:
                    what(row_copy(x, step, chan_at(-step), False))

        @pl.when(has_up)
        def _():
            for step in range(nchan):
                if own:
                    what(row_copy(x, step, chan, False))
                else:
                    what(row_copy(x, step, chan_at(-step), True))

    def start_exchange(x):
        on_rows(x, lambda c: c.start(), True)
        for step in range(1, nchan):
            block_copy(x, step, chan).start()

    def wait_row(x, step, slot, down):
        dst = 0 if down else rows + 1
        sem = (2 if down else 1) * nchan + step
        remote(
            ext.at[x, slot, pl.ds(dst, 1), mid], ext.at[x, slot, pl.ds(dst, 1), mid],
            x_send.at[x, sem], x_recv.at[x, sem],
            {"lat": lat - 1 if down else lat + 1, "chan": chan_at(-step)},
        ).wait_recv()

    def finish_middle(x):
        @pl.when(has_up)
        def _():
            for step in range(nchan):
                wait_row(x, step, chan_at(-step), True)

        @pl.when(has_down)
        def _():
            for step in range(nchan):
                wait_row(x, step, chan_at(-step), False)

        for step in range(1, nchan):
            block_copy(x, step, chan_at(-step)).wait_recv()
        col_copy(x, True).start()
        col_copy(x, False).start()

    def finish_columns(x):
        col_copy(x, True).wait_recv()
        col_copy(x, False).wait_recv()

    def finish_exchange(x):
        finish_middle(x)
        finish_columns(x)

    def end_exchange(x):
        on_rows(x, lambda c: c.wait_send(), True)
        for step in range(1, nchan):
            block_copy(x, step, chan).wait_send()
        col_copy(x, True).wait_send()
        col_copy(x, False).wait_send()

    half_w = width // nlon
    weights = (w1, w2)

    def weight_copy(which, step, peer, slot):
        return remote(
            weights[which].at[:, pl.ds(pl.multiple_of(peer * width + lon * half_w, half_w), half_w)],
            wb.at[which, :, pl.ds(pl.multiple_of(lon * half_w, half_w), half_w),
                  pl.ds(pl.multiple_of(slot * width, width), width)],
            w_send.at[which, step], w_recv.at[which, step], {"chan": chan_at(step)},
        )

    def forward_copy(which, step, hop, owner):
        at = (
            which, slice(None), pl.ds(pl.multiple_of(owner * half_w, half_w), half_w),
            pl.ds(pl.multiple_of(chan_at(-step) * width, width), width),
        )
        return remote(
            wb.at[at], wb.at[at], f_send.at[which, step, hop], f_recv.at[which, step, hop],
            {"lon": lon_at(hop)},
        )

    def pass_on(which):
        for step in range(1, nchan):
            weight_copy(which, step, chan, chan_at(-step)).wait_recv()
            for hop in range(1, nlon):
                forward_copy(which, step, hop, lon).start()

    def apply_filter(which, x, out):
        for i in range(rows):
            for slot in range(nchan):
                seen = ext[x, slot, i:i + 3].reshape(3 * wide, width)
                got = jnp.dot(band[which, i], seen, preferred_element_type=F32).astype(BF16)
                for k in range(KB):
                    out[i * cols:(i + 1) * cols,
                        k * channels + slot * width:k * channels + (slot + 1) * width] = got[
                            k * cols:(k + 1) * cols]

    def put(x, value):
        ext[x, chan, 1:rows + 1, mid] = value.reshape(rows, cols, width)

    def mix_back(which):
        total = None
        for k in range(KB):
            term = lax.dot_general(
                vb[:, k * channels:(k + 1) * channels], wb[which, k],
                (((1,), (1,)), ((), ())), preferred_element_type=F32,
            )
            total = term if total is None else total + term
        return total

    full_rows = KB * channels
    share = full_rows // nlon
    piece = share // chunks

    def rs_copy(g, step):
        return remote(
            rs_out.at[g, step - 1], rs_in.at[g, step - 1], rs_send.at[g, step - 1],
            rs_recv.at[g, step - 1], {"lon": lon_at(step)},
        )

    def weight_gradient(g, v, dpre):
        for k in range(KB):
            part[g, k * channels:(k + 1) * channels] = lax.dot_general(
                v[:, k * channels:(k + 1) * channels], dpre,
                (((0,), (0,)), ((), ())), preferred_element_type=F32,
            )
        for step in range(1, nlon):
            rs_out[g, step - 1] = part[
                g, pl.ds(pl.multiple_of(lon_at(step) * share, share), share)].astype(BF16)
            rs_copy(g, step).start()

    def chain_copy(j, right):
        out, into = (s_right, r_right) if right else (s_left, r_left)
        side = 0 if right else 1
        return remote(
            out.at[j], into.at[j], c_send.at[side, j], c_recv.at[side, j],
            {"lat": lat + 1 if right else lat - 1},
        )

    def chain_wait(j, right):
        into = r_right if right else r_left
        side = 0 if right else 1
        remote(
            into.at[j], into.at[j], c_send.at[side, j], c_recv.at[side, j],
            {"lat": lat - 1 if right else lat + 1},
        ).wait_recv()

    def ag_copy(j, step):
        return remote(
            ag_out.at[j], ag_in.at[step - 1, j], ag_send.at[step - 1, j],
            ag_recv.at[step - 1, j], {"lon": lon_at(step)},
        )

    def prepare(g):
        for step in range(1, nlon):
            rs_copy(g, step).wait_recv()
        own = part[g, pl.ds(pl.multiple_of(lon * share, share), share)]
        for step in range(1, nlon):
            own = own + rs_in[g, step - 1].astype(F32)
        tot[g * chunks:(g + 1) * chunks] = own.reshape(chunks, piece, width)

    rest = nlat - 1 - lat
    late = jnp.maximum(lat, rest)
    both = 2 * chunks

    def tick(time, carry):
        j_right = time - lat
        j_left = time - rest
        j_done = time - late
        do_right = (j_right >= 0) & (j_right < both)
        do_left = (j_left >= 0) & (j_left < both)

        @pl.when(do_right & (lat == 0))
        def _():
            s_right[j_right] = tot[j_right].astype(BF16)

        @pl.when(do_right & (lat > 0))
        def _():
            chain_wait(j_right, True)
            s_right[j_right] = (tot[j_right] + r_right[j_right].astype(F32)).astype(BF16)

        @pl.when(do_right & has_down)
        def _():
            chain_copy(j_right, True).start()

        @pl.when(do_left & (rest == 0))
        def _():
            s_left[j_left] = tot[j_left].astype(BF16)

        @pl.when(do_left & (rest > 0))
        def _():
            chain_wait(j_left, False)
            s_left[j_left] = (tot[j_left] + r_left[j_left].astype(F32)).astype(BF16)

        @pl.when(do_left & has_up)
        def _():
            chain_copy(j_left, False).start()

        @pl.when((j_done >= 0) & (j_done < both))
        def _():
            @pl.when(has_up)
            def _():
                tot[j_done] = tot[j_done] + r_right[j_done].astype(F32)

            @pl.when(has_down)
            def _():
                tot[j_done] = tot[j_done] + r_left[j_done].astype(F32)

            ag_out[j_done] = tot[j_done].astype(BF16)
            for step in range(1, nlon):
                ag_copy(j_done, step).start()

        return carry

    def settle():
        def one(j, carry):
            for step in range(1, nlon):
                ag_copy(j, step).wait_recv()
                ag_copy(j, step).wait_send()

            @pl.when(has_down)
            def _():
                chain_copy(j, True).wait_send()

            @pl.when(has_up)
            def _():
                chain_copy(j, False).wait_send()

            return carry

        lax.fori_loop(0, both, one, 0)
        for g, out in ((0, g2), (1, g1)):
            span = slice(g * chunks, (g + 1) * chunks)
            out[pl.ds(pl.multiple_of(lon * share, share), share)] = ag_out[span].reshape(share, width)
            for step in range(1, nlon):
                out[pl.ds(pl.multiple_of(lon_at(-step) * share, share), share)] = (
                    ag_in[step - 1, span].reshape(share, width)
                )
                rs_copy(g, step).wait_send()

    loads[0].wait()
    put(0, act[...])
    start_exchange(0)
    for load in loads[1:]:
        load.wait()
    build_band(0)
    build_band(1)
    for which in (1, 0):
        wb[which, :, :, pl.ds(pl.multiple_of(chan * width, width), width)] = weights[which][
            :, pl.ds(pl.multiple_of(chan * width, width), width)]
    finish_middle(0)
    for step in range(1, nchan):
        weight_copy(1, step, chan_at(step), chan).start()
    finish_columns(0)
    apply_filter(0, 0, v1)
    first = jnp.dot(v1[...], w1[...].reshape(full_rows, width), preferred_element_type=F32)
    pre1[...] = first
    hidden = (act[...].reshape(rows * cols, width).astype(F32) + gelu(first)).astype(BF16)
    put(1, hidden)
    start_exchange(1)
    pass_on(1)
    finish_middle(1)
    for step in range(1, nchan):
        weight_copy(0, step, chan_at(step), chan).start()
    finish_columns(1)
    apply_filter(0, 1, v2)
    second = jnp.dot(v2[...], w2[...].reshape(full_rows, width), preferred_element_type=F32)
    upstream = cot[...].reshape(rows * cols, width).astype(F32)
    dpre2 = (upstream * gelu_slope(second)).astype(BF16)
    put(2, dpre2)
    start_exchange(2)
    held = ext[1, chan, 1:rows + 1, mid].reshape(rows * cols, width).astype(F32)
    mixed[...] = (held + gelu(second)).astype(BF16).reshape(rows, cols, width)
    weight_gradient(0, v2, dpre2)
    pass_on(0)
    for which in (1, 0):
        for step in range(1, nchan):
            for hop in range(1, nlon):
                forward_copy(which, step, hop, lon_at(-hop)).wait_recv()
    prepare(0)
    lax.fori_loop(0, first_ticks, tick, 0)
    finish_exchange(2)
    apply_filter(1, 2, vb)
    back_hidden = (cot[...].reshape(rows * cols, width).astype(F32) + mix_back(1)).astype(BF16)
    back[...] = back_hidden
    dpre1 = (back_hidden.astype(F32) * gelu_slope(pre1[...])).astype(BF16)
    put(3, dpre1)
    start_exchange(3)
    weight_gradient(1, v1, dpre1)
    lax.fori_loop(first_ticks, chunks, tick, 0)
    prepare(1)
    lax.fori_loop(chunks, chunks + mid_ticks, tick, 0)
    finish_middle(3)
    lax.fori_loop(chunks + mid_ticks, nlat - 1 + both, tick, 0)
    finish_columns(3)
    apply_filter(1, 3, vb)
    gin[...] = (back[...].astype(F32) + mix_back(0)).reshape(rows, cols, width)
    settle()
    for x in range(4):
        end_exchange(x)
    for which in (1, 0):
        for step in range(1, nchan):
            weight_copy(which, step, chan_at(step), chan).wait_send()
            for hop in range(1, nlon):
                forward_copy(which, step, hop, lon).wait_send()


def body(sizes, activations, cotangent, w_first, w_second, offsets, basis, live, taps):
    nlat, nchan, nlon, chunks = sizes
    rows, cols, width = activations.shape
    channels = w_first.shape[1]
    wide = cols + 2 * EDGE
    table = coefficients(offsets, basis, live, taps).reshape(offsets.shape[0], 9 * KB)
    table = jnp.pad(table, ((HALO, HALO), (0, 0)))
    near = lax.dynamic_slice_in_dim(table, lax.axis_index("lat") * rows, rows + 2 * HALO, 0)
    full_rows = KB * channels
    share = full_rows // nlon
    piece = share // chunks
    cells = rows * cols
    dma = pltpu.SemaphoreType.DMA
    vmem = pl.BlockSpec(memory_space=pltpu.VMEM)
    slots = 3 * nchan + 2
    mixed, gin, g1, g2 = pl.pallas_call(
        functools.partial(kernel, sizes),
        out_shape=(
            jax.ShapeDtypeStruct((rows, cols, width), BF16),
            jax.ShapeDtypeStruct((rows, cols, width), F32),
            jax.ShapeDtypeStruct((full_rows, width), BF16),
            jax.ShapeDtypeStruct((full_rows, width), BF16),
        ),
        in_specs=[pl.BlockSpec(memory_space=pltpu.SMEM)] + [pl.BlockSpec(memory_space=pltpu.HBM)] * 4,
        out_specs=(vmem,) * 4,
        scratch_shapes=[
            pltpu.VMEM((rows, cols, width), BF16),
            pltpu.VMEM((rows, cols, width), BF16),
            pltpu.VMEM((KB, channels, width), BF16),
            pltpu.VMEM((KB, channels, width), BF16),
            pltpu.VMEM((4, nchan, rows + 2, wide, width), BF16),
            pltpu.VMEM((2, KB, width, channels), BF16),
            pltpu.VMEM((2, rows, KB * cols, 3 * wide), BF16),
            pltpu.VMEM((cells, full_rows), BF16),
            pltpu.VMEM((cells, full_rows), BF16),
            pltpu.VMEM((cells, full_rows), BF16),
            pltpu.VMEM((cells, width), F32),
            pltpu.VMEM((cells, width), BF16),
            pltpu.VMEM((2, full_rows, width), F32),
            pltpu.VMEM((2, nlon - 1, share, width), BF16),
            pltpu.VMEM((2, nlon - 1, share, width), BF16),
            pltpu.VMEM((2 * chunks, piece, width), F32),
            pltpu.VMEM((2 * chunks, piece, width), BF16),
            pltpu.VMEM((2 * chunks, piece, width), BF16),
            pltpu.VMEM((2 * chunks, piece, width), BF16),
            pltpu.VMEM((2 * chunks, piece, width), BF16),
            pltpu.VMEM((2 * chunks, piece, width), BF16),
            pltpu.VMEM((nlon - 1, 2 * chunks, piece, width), BF16),
            dma((4, slots)),
            dma((4, slots)),
            dma((2, nchan)),
            dma((2, nchan)),
            dma((2, nchan, nlon)),
            dma((2, nchan, nlon)),
            dma((2, nlon - 1)),
            dma((2, nlon - 1)),
            dma((2, 2 * chunks)),
            dma((2, 2 * chunks)),
            dma((nlon - 1, 2 * chunks)),
            dma((nlon - 1, 2 * chunks)),
            dma((4,)),
        ],
        compiler_params=pltpu.CompilerParams(
            collective_id=0, has_side_effects=True, vmem_limit_bytes=50 * 1024 * 1024
        ),
    )(near, activations, cotangent, w_first, w_second)
    shape = (KB, channels, width)
    return mixed, gin, g1.astype(F32).reshape(shape), g2.astype(F32).reshape(shape)


def solution(mesh):
    sizes = (mesh.shape["lat"], mesh.shape["chan"], mesh.shape["lon"], 2)
    return jax.shard_map(
        functools.partial(body, sizes),
        mesh=mesh,
        in_specs=(
            P(("groups", "lat"), "lon", "chan"),
            P(("groups", "lat"), "lon", "chan"),
            P(None, None, "chan"),
            P(None, None, "chan"),
            P(),
            P(),
            P(),
            P(),
        ),
        out_specs=(
            P(("groups", "lat"), "lon", "chan"),
            P(("groups", "lat"), "lon", "chan"),
            P("groups", None, "chan"),
            P("groups", None, "chan"),
        ),
        check_vma=False,
    )
```
